32 devices in a mesh: groups: 2 (over x), slide: 16 (over z, y, core).
Axes of the slice: x: 2, y: 2, z: 4, core: 2. Of those that a mesh axis runs over, the one named last changes fastest.
Arguments:
- tile_tokens: bfloat16 [24576, 1536], P(('groups', 'slide')), parts along dimension 0, may hold values from -6 to 6
- tile_counts: int32 [32], P('groups'), parts along dimension 0, may hold values from 1 to 3, 24 in all
- w_gate_up: bfloat16 [1536, 4096], replicated, may hold values from -0.15625 to 0.15625
- w_down: bfloat16 [2048, 1536], replicated, may hold values from -0.125 to 0.125
- w_tile_proj: bfloat16 [1536, 768], P('slide'), may hold values from -0.15625 to 0.15625
- slide_rows: bfloat16 [24576, 768], P(('groups', 'slide')), parts along dimension 0, may hold values from -6 to 6
- w_qkv: bfloat16 [768, 2304], P('slide'), may hold values from -5 to 5
- w_out: bfloat16 [768, 768], P('slide'), may hold values from -0.875 to 0.875
Outputs:
- slide_out: bfloat16 [24576, 768], P(('groups', 'slide')), parts along dimension 0
- tile_embeddings: bfloat16 [96, 1536], P(('groups', 'slide')), parts along dimension 0
The draws below stay inside these ranges and needn't reach their ends.
There are 2 independent parts, one for each index of `groups`. The reference program is written for one: setup_inputs(seed, part) draws one part's arguments, and reference() takes and returns one part's arrays. A program takes and returns all parts, laid end to end along the dimension named above; an argument that names none is the same for every part. Nothing has to cross between parts.
Inputs may be any that keep to these rules, and one draw needn't show every extreme that they name: `tile_counts`: each device's number of tiles; over the devices they sum to 24.
All inputs are finite; a program needn't handle non-finite values.
Results may differ from the reference program's by a relative error of at most 0.007.
The reference program's roundings to bfloat16 on the way count: a program that leaves them out, or rounds other values in their place, can miss the bound.
Values may be sent and summed in bfloat16 or wider, within the bound.
A program may use at most 192 MiB of HBM per device.

```python
import math
from functools import reduce
import jax
import jax.numpy as jnp
import numpy as np
from jax import lax

D = 1536
FF = 2048
TT = 256
BT = 32
TMAX = 3
HEADS = 16
HD = 48
DILATION = 4
L_DEV = 768
SD = 768
TILES = 24
SEQ = 12288
N_SLIDE = 16


def draw_w_qkv(key, part):
    key = jax.random.fold_in(key, 11)
    entries = jax.random.truncated_normal(key, -4.0, 4.0, (SD, 3 * SD), jnp.float32) * SD ** (-0.5)
    return entries.astype(jnp.bfloat16)


def steps_of(rng, extent, shards, low, top_value):
    level = 1.0
    for dim, shards_of in shards:
        heights = jax.random.uniform(jax.random.fold_in(jax.random.fold_in(rng, 6), dim), (shards_of,), jnp.float32, low / len(shards), top_value / len(shards))
        level = level * jnp.repeat(jnp.exp(heights), extent[dim] // shards_of).reshape((-1,) + (1,) * (len(extent) - 1 - dim))
    return level


def profile(count, total, most, slope):
    loads = [(1 << 20) // math.isqrt(grade ** slope) + 1 for grade in range(2, count + 1)]
    spare, counts = total - most - (count - 1), [1] * (count - 1)
    while spare > 0:
        candidates = [i for i in range(count - 1) if counts[i] < most]
        mass, remaining = sum([loads[i] for i in candidates]), spare
        for i in candidates:
            extra = min(most - counts[i], max(1, remaining * loads[i] // mass), spare)
            counts[i] = counts[i] + extra
            spare = spare - extra
    return np.array([most] + counts)


def uneven_parts(stream_key, number_of, total, limit, lean):
    if number_of == 2:
        one = jax.random.randint(stream_key, (), max(1, total - limit), min(limit, total - 1) + 1)
        return jnp.stack([one, total - one])
    tallies = jnp.asarray(profile(number_of, total, limit, lean), jnp.int32)
    couples = (number_of - 1) // 2
    giver, sink = tallies[1:1 + 2 * couples:2], tallies[2:2 + 2 * couples:2]
    slack = jnp.minimum(giver - 1, limit - sink)
    moved = jax.random.randint(jax.random.fold_in(stream_key, 1), (couples,), 0, 1 << 20) % (slack + 1)
    tallies = tallies.at[1:1 + 2 * couples:2].set(giver - moved).at[2:2 + 2 * couples:2].set(sink + moved)
    return tallies[jax.random.permutation(jax.random.fold_in(stream_key, 2), number_of)]


def gaussian(stream_key, dims, deviation, limit, shards=(), held_as=jnp.bfloat16):
    factor_of = steps_of(stream_key, dims, shards, -0.22, 0.18) if shards else 1.0
    result = jax.random.normal(stream_key, dims, jnp.float32) * deviation * factor_of
    return jnp.minimum(jnp.maximum(result, -limit), limit).astype(held_as)


def setup_inputs(seed: int = 0, part: int = 0) -> dict:
    streams_of = jax.random.split(jax.random.key(seed), 9)
    part_splits = jax.random.split(jax.random.fold_in(streams_of[8], part), 9)
    tile_tokens = gaussian(part_splits[0], (N_SLIDE * TMAX * TT, D), 1.0, 6.0, ((0, 16),))
    tile_counts = uneven_parts(part_splits[1], N_SLIDE, TMAX * N_SLIDE // 2, TMAX, 2).astype(jnp.int32)
    w_gate_up = gaussian(streams_of[2], (D, 2 * FF), D ** -0.5, 0.15625)
    w_down = gaussian(streams_of[3], (FF, D), FF ** -0.5, 0.125)
    w_tile_proj = gaussian(streams_of[4], (D, SD), D ** -0.5, 0.15625, ((0, 16),))
    slide_rows = gaussian(part_splits[5], (SEQ, SD), 1.0, 6.0, ((0, 16),))
    w_qkv = draw_w_qkv(jax.random.fold_in(streams_of[8], 71), part)
    w_out = gaussian(streams_of[7], (SD, SD), (SD // 16) ** -0.5, 0.875, ((0, 16),))
    return dict(tile_tokens=tile_tokens, tile_counts=tile_counts, w_gate_up=w_gate_up, w_down=w_down, w_tile_proj=w_tile_proj, slide_rows=slide_rows, w_qkv=w_qkv, w_out=w_out)


tile_epsilon = 1e-06
slide_epsilon = 1e-05
far_below = -1e+30

def normalize(matrix, epsilon):
    average = lax.optimization_barrier(jnp.mean(matrix, axis=-1, keepdims=True))
    centered = matrix - average
    variance = lax.optimization_barrier(jnp.mean(centered * centered, axis=-1, keepdims=True))
    return centered * lax.rsqrt(variance + epsilon)

def attend(queries, key_rows, value_rows):
    scores = jnp.dot(queries, key_rows.T, preferred_element_type=jnp.float32) * HD ** (-0.5)
    row_peak = lax.optimization_barrier(jnp.max(scores, axis=1, keepdims=True))
    weights = jnp.exp(scores - row_peak)
    row_total = lax.optimization_barrier(jnp.sum(weights, axis=1, keepdims=True))
    weighted = jnp.dot(weights.astype(jnp.bfloat16), value_rows, preferred_element_type=jnp.float32)
    return (weighted / row_total, (row_peak + jnp.log(row_total))[:, 0])

def attend_heads(queries, key_rows, value_rows):
    outputs, lse_rows = lax.map(lambda triple: attend(triple[0], triple[1], triple[2]), (jnp.swapaxes(queries, 0, 1), jnp.swapaxes(key_rows, 0, 1), jnp.swapaxes(value_rows, 0, 1)))
    return (jnp.swapaxes(outputs, 0, 1), jnp.swapaxes(lse_rows, 0, 1))

def mixed_sums(token_blocks, w_gate_up, w_down):
    block_count = token_blocks.shape[0]
    flat_rows = token_blocks.reshape(-1, token_blocks.shape[2]).astype(jnp.float32)
    normed = normalize(flat_rows, tile_epsilon).astype(jnp.bfloat16)
    gate_up = jnp.dot(normed, w_gate_up, preferred_element_type=jnp.float32)
    hidden_width = w_down.shape[0]
    hidden = (jax.nn.silu(gate_up[:, :hidden_width]) * gate_up[:, hidden_width:]).astype(jnp.bfloat16)
    mixed = jnp.dot(hidden, w_down, preferred_element_type=jnp.float32)
    return lax.optimization_barrier(jnp.sum(mixed.reshape(block_count, -1, mixed.shape[1]), axis=1))

def pick_every(field_rows, stride):
    head_count = field_rows.shape[1]
    field_grid = field_rows.reshape(field_rows.shape[0] // stride, stride, head_count, field_rows.shape[2])
    head_phase = (jnp.arange(head_count) % stride)[None, :, None]
    chosen = field_grid[:, 0]
    for phase in range(1, stride):
        chosen = jnp.where(head_phase == phase, field_grid[:, phase], chosen)
    return chosen

def spread_every(branch_out, branch_lse, stride):
    head_count = branch_out.shape[1]
    matches = jnp.arange(stride)[:, None] == (jnp.arange(head_count) % stride)[None, :]
    out_grid = jnp.where(matches[None, :, :, None], branch_out[:, None], 0.0)
    lse_grid = jnp.where(matches[None], branch_lse[:, None], far_below)
    return (out_grid.reshape(-1, head_count, branch_out.shape[2]), lse_grid.reshape(-1, head_count))

def combine(branches):
    highest = reduce(jnp.maximum, [branch[1] for branch in branches])
    weights = [jnp.exp(branch[1] - highest) for branch in branches]
    numerator = reduce(jnp.add, [weight[:, :, None] * branch[0] for weight, branch in zip(weights, branches)])
    denominator = reduce(jnp.add, weights)
    return numerator / denominator[:, :, None]

def reference(tile_tokens, tile_counts, w_gate_up, w_down, w_tile_proj, slide_rows, w_qkv, w_out):
    slot_count = N_SLIDE * TMAX
    per_tile = TT // BT
    valid_slot = jnp.arange(TMAX, dtype=jnp.int32)[None, :] < tile_counts[:, None]
    flat_valid = valid_slot.reshape(-1).astype(jnp.int32)
    tile_order = jnp.argsort(1 - flat_valid, stable=True)[:TILES].astype(jnp.int32)
    tile_rows = tile_tokens.reshape(slot_count, TT, D)[tile_order]

    def encode(one_tile):
        block_sums = mixed_sums(one_tile.reshape(per_tile, BT, D), w_gate_up, w_down)
        return (lax.optimization_barrier(jnp.sum(one_tile.astype(jnp.float32), axis=0)) + lax.optimization_barrier(jnp.sum(block_sums, axis=0))) / TT
    pooled = lax.map(encode, tile_rows)
    embedded = normalize(pooled, tile_epsilon).astype(jnp.bfloat16)
    tile_embeddings = jnp.zeros((slot_count, D), jnp.bfloat16).at[tile_order].set(embedded)
    fresh_rows = jnp.dot(embedded, w_tile_proj, preferred_element_type=jnp.float32).astype(jnp.bfloat16)
    placed = jnp.zeros((slot_count, SD), jnp.bfloat16).at[tile_order].set(fresh_rows).reshape(N_SLIDE, TMAX, SD)
    blocks_now = slide_rows.reshape(N_SLIDE, L_DEV, SD)
    head_rows = jnp.where(valid_slot[:, :, None], placed, blocks_now[:, :TMAX])
    slide_now = jnp.concatenate([head_rows, blocks_now[:, TMAX:]], axis=1).reshape(SEQ, SD)
    normed = normalize(slide_now.astype(jnp.float32), slide_epsilon).astype(jnp.bfloat16)
    projected = jnp.dot(normed, w_qkv, preferred_element_type=jnp.float32).astype(jnp.bfloat16)
    queries = projected[:, :SD].reshape(SEQ, HEADS, HD)
    key_rows = projected[:, SD:2 * SD].reshape(SEQ, HEADS, HD)
    value_rows = projected[:, 2 * SD:].reshape(SEQ, HEADS, HD)

    def per_segment(triple):
        return attend_heads(triple[0], triple[1], triple[2])

    def segments(field_rows, count):
        return field_rows.reshape(count, -1, HEADS, HD)
    local_out, local_lse = lax.map(per_segment, (segments(queries, N_SLIDE), segments(key_rows, N_SLIDE), segments(value_rows, N_SLIDE)))
    local_out = local_out.reshape(SEQ, HEADS, HD)
    local_lse = local_lse.reshape(SEQ, HEADS)
    pair_count = N_SLIDE // 2
    pair_out, pair_lse = lax.map(per_segment, (segments(pick_every(queries, 2), pair_count), segments(pick_every(key_rows, 2), pair_count), segments(pick_every(value_rows, 2), pair_count)))
    pair_out, pair_lse = spread_every(pair_out.reshape(SEQ // 2, HEADS, HD), pair_lse.reshape(SEQ // 2, HEADS), 2)
    wide_out, wide_lse = attend_heads(pick_every(queries, DILATION), pick_every(key_rows, DILATION), pick_every(value_rows, DILATION))
    wide_out, wide_lse = spread_every(wide_out, wide_lse, DILATION)
    attended = combine([(local_out, local_lse), (pair_out, pair_lse), (wide_out, wide_lse)]).reshape(SEQ, SD).astype(jnp.bfloat16)
    slide_out = (slide_now.astype(jnp.float32) + jnp.dot(attended, w_out, preferred_element_type=jnp.float32)).astype(jnp.bfloat16)
    return (slide_out, tile_embeddings)
```

```python
import functools
import math

import jax
import jax.numpy as jnp
import numpy as np
from jax import lax
from jax.experimental import pallas as pl
from jax.experimental.pallas import tpu as pltpu
from jax.sharding import PartitionSpec as P

TT = 256
TMAX = 3
HEADS = 16
HD = 48
DILATION = 4
LANES = 128

tile_epsilon = 1e-06
slide_epsilon = 1e-05
SCALE = HD ** (-0.5) * math.log2(math.e)
BLOCK_OF = {0: 0, 2: 1, 1: 2, 3: 3}

f32 = jnp.float32
bf16 = jnp.bfloat16
VMEM = pl.BlockSpec(memory_space=pltpu.VMEM)
SMEM = pl.BlockSpec(memory_space=pltpu.SMEM)
PARAMS = pltpu.CompilerParams(vmem_limit_bytes=56 * 1024 * 1024)


def normalize(matrix, epsilon):
    average = jnp.mean(matrix, axis=-1, keepdims=True)
    centered = matrix - average
    variance = jnp.mean(centered * centered, axis=-1, keepdims=True)
    return centered * lax.rsqrt(variance + epsilon)


def dot(a, b):
    return jnp.dot(a, b, preferred_element_type=f32)


def dot_nt(a, b):
    return lax.dot_general(a, b, (((1,), (1,)), ((), ())), preferred_element_type=f32)


def split3(value):
    high = value.astype(bf16)
    rest = value - high.astype(f32)
    middle = rest.astype(bf16)
    return high, middle, (rest - middle.astype(f32)).astype(bf16)


def window(head):
    first = head * HD
    start = first // LANES * LANES
    width = LANES if first + HD <= start + LANES else 2 * LANES
    return start, width, first - start


def lane_mask(width, offset):
    lane = lax.broadcasted_iota(jnp.int32, (1, width), 1)
    return (lane >= offset) & (lane < offset + HD)


def permutation(rows, transposed):
    each = rows // DILATION
    stored = lax.broadcasted_iota(jnp.int32, (rows, rows), 1 if transposed else 0)
    position = lax.broadcasted_iota(jnp.int32, (rows, rows), 0 if transposed else 1)
    block = sum((stored >= each * i).astype(jnp.int32) for i in range(1, DILATION))
    phase = jnp.where(block == 1, 2, jnp.where(block == 2, 1, block))
    wanted = (stored - block * each) * DILATION + phase
    return jnp.where(position == wanted, 1.0, 0.0).astype(bf16)


def tile_kernel(count_ref, tokens_ref, gate_ref, up_ref, down_ref, out_ref, normed, mixed):
    step = pl.program_id(0)

    @pl.when(step == 0)
    def _():
        mixed[...] = jnp.zeros_like(mixed)
        for slot in range(TMAX):
            rows = pl.ds(slot * TT, TT)
            tokens = tokens_ref[rows, :].astype(f32)
            normed[rows, :] = normalize(tokens, tile_epsilon).astype(bf16)
            mixed[slot : slot + 1, :] = jnp.sum(tokens, axis=0, keepdims=True)

    for slot in range(TMAX):

        @pl.when(slot < count_ref[0])
        def _():
            rows = normed[pl.ds(slot * TT, TT), :]
            gate = dot(rows, gate_ref[...])
            up = dot(rows, up_ref[...])
            hidden = (gate * jax.nn.sigmoid(gate) * up).astype(bf16).astype(f32)
            total = jnp.broadcast_to(jnp.sum(hidden, axis=0, keepdims=True), (8, hidden.shape[1]))
            parts = split3(total)
            down = down_ref[...]
            add = dot(parts[0], down) + dot(parts[1], down) + dot(parts[2], down)
            mixed[slot : slot + 1, :] += add[:1]

    @pl.when(step == pl.num_programs(0) - 1)
    def _():
        out_ref[...] = normalize(mixed[...] / TT, tile_epsilon).astype(bf16)


def encode_tiles(my_count, tile_tokens, w_gate_up, w_down):
    rows, width = tile_tokens.shape
    hidden = w_down.shape[0]
    block = 512
    steps = hidden // block
    return pl.pallas_call(
        tile_kernel,
        grid=(steps,),
        out_shape=jax.ShapeDtypeStruct((16, width), bf16),
        in_specs=[
            SMEM,
            pl.BlockSpec((rows, width), lambda i: (0, 0)),
            pl.BlockSpec((width, block), lambda i: (0, i)),
            pl.BlockSpec((width, block), lambda i: (0, i + steps)),
            pl.BlockSpec((block, width), lambda i: (i, 0)),
        ],
        out_specs=pl.BlockSpec((16, width), lambda i: (0, 0)),
        scratch_shapes=[pltpu.VMEM((rows, width), bf16), pltpu.VMEM((16, width), f32)],
        compiler_params=PARAMS,
        cost_estimate=pl.CostEstimate(
            flops=2 * rows * width * 2 * hidden, bytes_accessed=22 * 1024 * 1024, transcendentals=0
        ),
        name="tile_block",
    )(my_count, tile_tokens, w_gate_up, w_gate_up, w_down)


def project_kernel(
    repeat, count_ref, emb_ref, proj_ref, rows_ref, qkv_ref, now_ref, q_ref, k_ref, v_ref, far_ref, send_ref
):
    rows, width = rows_ref.shape
    each, half = rows // DILATION, rows // 2
    fresh = dot(emb_ref[...], proj_ref[...]).astype(bf16).astype(f32)
    keep = lax.broadcasted_iota(jnp.int32, (16, 1), 0) < count_ref[0]
    now_ref[...] = rows_ref[...]
    now_ref[0:16, :] = jnp.where(keep, fresh, rows_ref[0:16, :].astype(f32)).astype(bf16)
    normed = normalize(now_ref[...].astype(f32), slide_epsilon).astype(bf16)
    normed = dot(permutation(rows, False), normed).astype(bf16)
    for index, ref in enumerate((q_ref, k_ref, v_ref)):
        ref[...] = dot(normed, qkv_ref[:, index * width : (index + 1) * width]).astype(bf16)
    lane = lax.broadcasted_iota(jnp.int32, (1, width), 1)
    head = sum((lane >= HD * i).astype(jnp.int32) for i in range(1, HEADS))
    even = (head & 1) == 0
    for index, ref in enumerate((k_ref, v_ref)):
        far_ref[index * half : (index + 1) * half, :] = jnp.where(
            even, ref[0:half, :].astype(f32), ref[half:rows, :].astype(f32)
        ).astype(bf16)
    tail_rows = each // 8
    for h in range(HEADS):
        first = BLOCK_OF[h % DILATION] * each
        pieces = [
            ref[first : first + each, h * HD : (h + 1) * HD].astype(f32)
            for ref in (q_ref, k_ref, v_ref)
        ]
        main = jnp.concatenate([pieces[0], pieces[1], pieces[2][:, :32]], axis=1)
        tail = jnp.concatenate(
            [pieces[2][r * tail_rows : (r + 1) * tail_rows, 32:] for r in range(8)], axis=1
        )
        whole = jnp.concatenate([main, tail], axis=0).astype(bf16)
        for again in range(repeat):
            send_ref[h * repeat + again] = whole


def project(repeat, my_count, embedded, proj_full, slide_rows, qkv_full):
    rows, width = slide_rows.shape
    each = rows // DILATION
    square = jax.ShapeDtypeStruct((rows, width), bf16)
    return pl.pallas_call(
        functools.partial(project_kernel, repeat),
        out_shape=[square] * 5
        + [jax.ShapeDtypeStruct((HEADS * repeat, each + each // 8, LANES), bf16)],
        in_specs=[SMEM] + [VMEM] * 4,
        out_specs=[VMEM] * 6,
        compiler_params=PARAMS,
        cost_estimate=pl.CostEstimate(
            flops=2 * rows * width * 4 * width, bytes_accessed=16 * 1024 * 1024, transcendentals=0
        ),
        name="project",
    )(my_count, embedded, proj_full, slide_rows, qkv_full)


def near_kernel(q_ref, k_ref, v_ref, far_ref, out_ref, lse_ref):
    rows = q_ref.shape[0]
    half = rows // 2
    chunk = 128
    for h in range(8):
        start, width, offset = window(h)
        lanes = slice(start, start + width)
        mask = lane_mask(width, offset)
        outside = 0 if offset > 0 else HD
        parity = h % 2
        same = slice(parity * half, parity * half + half)
        other = slice((1 - parity) * half, (1 - parity) * half + half)

        def ones_outside(value):
            return jnp.where(mask, value.astype(f32), 1.0).astype(bf16)

        keys_same, keys_other, keys_far = k_ref[same, lanes], k_ref[other, lanes], far_ref[:half, lanes]
        values_same = ones_outside(v_ref[same, lanes])
        values_other = ones_outside(v_ref[other, lanes])
        values_far = ones_outside(far_ref[half:, lanes])
        for part in range(rows // chunk):
            at = slice(part * chunk, (part + 1) * chunk)
            in_pair = same.start <= at.start < same.stop
            queries = jnp.where(mask, q_ref[at, lanes].astype(f32), 0.0).astype(bf16)
            scores = [dot_nt(queries, keys_same), dot_nt(queries, keys_other)]
            values = [values_same, values_other]
            if in_pair:
                scores.append(dot_nt(queries, keys_far))
                values.append(values_far)
            peaks = [jnp.max(s, axis=1, keepdims=True) for s in scores]
            peak = functools.reduce(jnp.maximum, peaks) * SCALE
            total = 0.0
            for index, (s, v) in enumerate(zip(scores, values)):
                shift = peak - 1.0 if in_pair and index == 0 else peak
                total = total + dot(jnp.exp2(s * SCALE - shift).astype(bf16), v)
            mass = total[:, outside : outside + 1]
            out_ref[at, lanes] = jnp.where(mask, total * (1.0 / mass), out_ref[at, lanes])
            lse_ref[at, lanes] = jnp.where(mask, peak + jnp.log2(mass), lse_ref[at, lanes])


def attend_near(queries, key_rows, value_rows, far):
    rows, width = queries.shape
    spec = pl.BlockSpec((rows, 8 * HD), lambda i: (0, i))
    return pl.pallas_call(
        near_kernel,
        grid=(width // (8 * HD),),
        out_shape=[jax.ShapeDtypeStruct((rows, width), f32)] * 2,
        in_specs=[spec] * 4,
        out_specs=[spec] * 2,
        compiler_params=PARAMS,
        cost_estimate=pl.CostEstimate(
            flops=12 * 10**9, bytes_accessed=10 * 1024 * 1024, transcendentals=12 * 10**6
        ),
        name="near_attention",
    )(queries, key_rows, value_rows, far)


def wide_kernel(repeat, part_ref, recv_ref, out_ref, keys, values):
    count, packed, _ = recv_ref.shape
    each = packed * 8 // 9
    tail_rows = each // 8
    lane = lax.broadcasted_iota(jnp.int32, (1, LANES), 1)
    step = pl.program_id(0)

    @pl.when(step == 0)
    def _():
        @pl.loop(0, count)
        def _(source):
            block = recv_ref[source]
            at = pl.ds(pl.multiple_of(source * each, each), each)
            keys[at, :] = block[:each]
            wide = block.astype(f32)
            tail = wide[each:]
            tails = [tail] + [pltpu.roll(tail, LANES - 16 * r, axis=1) for r in range(1, 8)]
            tail = jnp.concatenate(tails, axis=0)
            picked = jnp.where(lane >= 96, wide[:each], jnp.where(lane < 16, tail, 1.0))
            values[at, :] = picked.astype(bf16)

    queries = pltpu.roll(recv_ref[step * repeat + part_ref[0]].astype(f32)[:each], HD, axis=1)
    queries = jnp.where((lane >= HD) & (lane < 2 * HD), queries, 0.0).astype(bf16)
    scores = dot_nt(queries, keys[...])
    peak = jnp.max(scores, axis=1, keepdims=True) * SCALE
    total = dot(jnp.exp2(scores * SCALE - peak).astype(bf16), values[...])
    total = pltpu.roll(total, 32, axis=1)
    mass = total[:, HD : HD + 1]
    lse = peak + jnp.log2(mass)
    high, middle, low = [piece.astype(f32) for piece in split3(lse)]
    out = jnp.where(
        lane < HD,
        total * (1.0 / mass),
        jnp.where(lane == HD, high, jnp.where(lane == HD + 1, middle, low)),
    )
    upper = pltpu.roll(out[each // 2 :], 64, axis=1)
    out_ref[0] = jnp.where(lane < 64, out[: each // 2], upper).astype(bf16)


def attend_wide(repeat, part, received):
    count, packed, _ = received.shape
    each = packed * 8 // 9
    steps = count // repeat
    return pl.pallas_call(
        functools.partial(wide_kernel, repeat),
        grid=(steps,),
        out_shape=jax.ShapeDtypeStruct((steps, each // 2, LANES), bf16),
        in_specs=[SMEM, pl.BlockSpec(received.shape, lambda i: (0, 0, 0))],
        out_specs=pl.BlockSpec((1, each // 2, LANES), lambda i: (i, 0, 0)),
        scratch_shapes=[pltpu.VMEM((count * each, LANES), bf16)] * 2,
        compiler_params=PARAMS,
        cost_estimate=pl.CostEstimate(
            flops=10 * 10**9, bytes_accessed=2 * 1024 * 1024, transcendentals=10**7
        ),
        name="wide_attention",
    )(part, received)


def finish_kernel(near_ref, lse_ref, wide_ref, out_w_ref, now_ref, out_ref, mixed):
    rows, width = near_ref.shape
    each = rows // DILATION
    mixed[...] = near_ref[...]
    for h in range(HEADS):
        start, span, offset = window(h)
        lanes = slice(start, start + span)
        mask = lane_mask(span, offset)
        first = BLOCK_OF[h % DILATION] * each
        at = slice(first, first + each)
        block = wide_ref[h].astype(f32)
        block = jnp.concatenate([block, pltpu.roll(block, 64, axis=1)], axis=0)
        far_lse = block[:, HD : HD + 1] + block[:, HD + 1 : HD + 2] + block[:, HD + 2 : HD + 3]
        if span > LANES:
            block = jnp.concatenate([block, jnp.zeros_like(block)], axis=1)
        far_out = pltpu.roll(block, offset, axis=1) if offset else block
        near_lse = jnp.where(mask, lse_ref[at, lanes], 0.0)
        highest = jnp.maximum(near_lse, far_lse)
        near_weight, far_weight = jnp.exp2(near_lse - highest), jnp.exp2(far_lse - highest)
        merged = (near_weight * near_ref[at, lanes] + far_weight * far_out) / (near_weight + far_weight)
        mixed[at, lanes] = jnp.where(mask, merged, mixed[at, lanes])
    attended = dot(permutation(rows, True), mixed[...].astype(bf16)).astype(bf16)
    out_ref[...] = (now_ref[...].astype(f32) + dot(attended, out_w_ref[...])).astype(bf16)


def finish(near_out, near_lse, wide, out_full, slide_now):
    rows, width = slide_now.shape
    return pl.pallas_call(
        finish_kernel,
        out_shape=jax.ShapeDtypeStruct((rows, width), bf16),
        in_specs=[VMEM] * 5,
        out_specs=VMEM,
        scratch_shapes=[pltpu.VMEM((rows, width), f32)],
        compiler_params=PARAMS,
        cost_estimate=pl.CostEstimate(
            flops=4 * rows * width * width, bytes_accessed=9 * 1024 * 1024, transcendentals=0
        ),
        name="finish",
    )(near_out, near_lse, wide, out_full, slide_now)


def body(tile_tokens, tile_counts, w_gate_up, w_down, w_tile_proj, slide_rows, w_qkv, w_out):
    size = lax.axis_size("slide")
    repeat = size // HEADS
    me = lax.axis_index("slide")
    my_count = lax.dynamic_slice(tile_counts, (me,), (1,))
    qkv_full = lax.all_gather(w_qkv, "slide", axis=0, tiled=True)
    proj_full = lax.all_gather(w_tile_proj, "slide", axis=0, tiled=True)
    out_full = lax.all_gather(w_out, "slide", axis=0, tiled=True)
    embedded = encode_tiles(my_count, tile_tokens, w_gate_up, w_down)
    keep = jnp.arange(TMAX, dtype=jnp.int32)[:, None] < my_count
    tile_embeddings = jnp.where(keep, embedded[:TMAX], jnp.zeros((), bf16))
    slide_now, queries, key_rows, value_rows, far, send = project(
        repeat, my_count, embedded, proj_full, slide_rows, qkv_full
    )
    far = lax.ppermute(far, "slide", [(source, source ^ 1) for source in range(size)])
    received = lax.all_to_all(send, "slide", 0, 0, tiled=True)
    near_out, near_lse = attend_near(queries, key_rows, value_rows, far)
    wide = attend_wide(repeat, (me % repeat).astype(jnp.int32)[None], received)
    wide = jnp.repeat(wide, repeat, axis=0) if repeat > 1 else wide
    wide = lax.all_to_all(wide, "slide", 0, 0, tiled=True)
    if repeat > 1:
        wide = lax.dynamic_index_in_dim(
            wide.reshape(HEADS, repeat, *wide.shape[1:]), me % repeat, 1, keepdims=False
        )
    return finish(near_out, near_lse, wide, out_full, slide_now), tile_embeddings


def solution(mesh):
    return jax.shard_map(
        body,
        mesh=mesh,
        in_specs=(
            P(("groups", "slide"), None),
            P("groups"),
            P(),
            P(),
            P("slide", None),
            P(("groups", "slide"), None),
            P("slide", None),
            P("slide", None),
        ),
        out_specs=(P(("groups", "slide"), None), P(("groups", "slide"), None)),
        check_vma=False,
    )
```

```python
import functools
import math

import jax
import jax.numpy as jnp
import numpy as np
from jax import lax
from jax.experimental import pallas as pl
from jax.experimental.pallas import tpu as pltpu
from jax.sharding import PartitionSpec as P

TT = 256
TMAX = 3
HEADS = 16
HD = 48
DILATION = 4
LANES = 128

tile_epsilon = 1e-06
slide_epsilon = 1e-05
SCALE = HD ** (-0.5) * math.log2(math.e)
BLOCK_OF = {0: 0, 2: 1, 1: 2, 3: 3}

f32 = jnp.float32
bf16 = jnp.bfloat16
VMEM = pl.BlockSpec(memory_space=pltpu.VMEM)
SMEM = pl.BlockSpec(memory_space=pltpu.SMEM)
PARAMS = pltpu.CompilerParams(vmem_limit_bytes=56 * 1024 * 1024)


def normalize(matrix, epsilon):
    average = jnp.mean(matrix, axis=-1, keepdims=True)
    centered = matrix - average
    variance = jnp.mean(centered * centered, axis=-1, keepdims=True)
    return centered * lax.rsqrt(variance + epsilon)


def dot(a, b):
    return jnp.dot(a, b, preferred_element_type=f32)


def dot_nt(a, b):
    return lax.dot_general(a, b, (((1,), (1,)), ((), ())), preferred_element_type=f32)


def split3(value):
    high = value.astype(bf16)
    rest = value - high.astype(f32)
    middle = rest.astype(bf16)
    return high, middle, (rest - middle.astype(f32)).astype(bf16)


def window(head):
    first = head * HD
    start = first // LANES * LANES
    width = LANES if first + HD <= start + LANES else 2 * LANES
    return start, width, first - start


def lane_mask(width, offset):
    lane = lax.broadcasted_iota(jnp.int32, (1, width), 1)
    return (lane >= offset) & (lane < offset + HD)


def permutation(rows, transposed):
    each = rows // DILATION
    stored = lax.broadcasted_iota(jnp.int32, (rows, rows), 1 if transposed else 0)
    position = lax.broadcasted_iota(jnp.int32, (rows, rows), 0 if transposed else 1)
    block = sum((stored >= each * i).astype(jnp.int32) for i in range(1, DILATION))
    phase = jnp.where(block == 1, 2, jnp.where(block == 2, 1, block))
    wanted = (stored - block * each) * DILATION + phase
    return jnp.where(position == wanted, 1.0, 0.0).astype(bf16)


def tile_kernel(count_ref, tokens_ref, gate_ref, up_ref, down_ref, out_ref, normed, mixed):
    step = pl.program_id(0)

    @pl.when(step == 0)
    def _():
        mixed[...] = jnp.zeros_like(mixed)
        for slot in range(TMAX):
            rows = pl.ds(slot * TT, TT)
            tokens = tokens_ref[rows, :].astype(f32)
            normed[rows, :] = normalize(tokens, tile_epsilon).astype(bf16)
            mixed[slot : slot + 1, :] = jnp.sum(tokens, axis=0, keepdims=True)

    for slot in range(TMAX):

        @pl.when(slot < count_ref[0])
        def _():
            rows = normed[pl.ds(slot * TT, TT), :]
            gate = dot(rows, gate_ref[...])
            up = dot(rows, up_ref[...])
            hidden = (gate * jax.nn.sigmoid(gate) * up).astype(bf16).astype(f32)
            total = jnp.broadcast_to(jnp.sum(hidden, axis=0, keepdims=True), (8, hidden.shape[1]))
            parts = split3(total)
            down = down_ref[...]
            add = dot(parts[0], down) + dot(parts[1], down) + dot(parts[2], down)
            mixed[slot : slot + 1, :] += add[:1]

    @pl.when(step == pl.num_programs(0) - 1)
    def _():
        out_ref[...] = normalize(mixed[...] / TT, tile_epsilon).astype(bf16)


def encode_tiles(my_count, tile_tokens, w_gate_up, w_down):
    rows, width = tile_tokens.shape
    hidden = w_down.shape[0]
    block = 512
    steps = hidden // block
    return pl.pallas_call(
        tile_kernel,
        grid=(steps,),
        out_shape=jax.ShapeDtypeStruct((16, width), bf16),
        in_specs=[
            SMEM,
            pl.BlockSpec((rows, width), lambda i: (0, 0)),
            pl.BlockSpec((width, block), lambda i: (0, i)),
            pl.BlockSpec((width, block), lambda i: (0, i + steps)),
            pl.BlockSpec((block, width), lambda i: (i, 0)),
        ],
        out_specs=pl.BlockSpec((16, width), lambda i: (0, 0)),
        scratch_shapes=[pltpu.VMEM((rows, width), bf16), pltpu.VMEM((16, width), f32)],
        compiler_params=PARAMS,
        cost_estimate=pl.CostEstimate(
            flops=2 * rows * width * 2 * hidden, bytes_accessed=22 * 1024 * 1024, transcendentals=0
        ),
        name="tile_block",
    )(my_count, tile_tokens, w_gate_up, w_gate_up, w_down)


def project_kernel(
    repeat, count_ref, emb_ref, proj_ref, rows_ref, qkv_ref, now_ref, q_ref, k_ref, v_ref, far_ref, send_ref
):
    rows, width = rows_ref.shape
    each, half = rows // DILATION, rows // 2
    fresh = dot(emb_ref[0], proj_ref[:, :width]) + dot(emb_ref[1], proj_ref[:, width:])
    fresh = fresh.astype(bf16).astype(f32)
    keep = lax.broadcasted_iota(jnp.int32, (16, 1), 0) < count_ref[0]
    now_ref[...] = rows_ref[...]
    now_ref[0:16, :] = jnp.where(keep, fresh, rows_ref[0:16, :].astype(f32)).astype(bf16)
    normed = normalize(now_ref[...].astype(f32), slide_epsilon).astype(bf16)
    normed = dot(permutation(rows, False), normed).astype(bf16)
    for index, ref in enumerate((q_ref, k_ref, v_ref)):
        ref[...] = dot(normed, qkv_ref[:, index * width : (index + 1) * width]).astype(bf16)
    lane = lax.broadcasted_iota(jnp.int32, (1, width), 1)
    head = sum((lane >= HD * i).astype(jnp.int32) for i in range(1, HEADS))
    even = (head & 1) == 0
    for index, ref in enumerate((k_ref, v_ref)):
        far_ref[index * half : (index + 1) * half, :] = jnp.where(
            even, ref[0:half, :].astype(f32), ref[half:rows, :].astype(f32)
        ).astype(bf16)
    tail_rows = each // 8
    for h in range(HEADS):
        first = BLOCK_OF[h % DILATION] * each
        pieces = [
            ref[first : first + each, h * HD : (h + 1) * HD].astype(f32)
            for ref in (q_ref, k_ref, v_ref)
        ]
        main = jnp.concatenate([pieces[0], pieces[1], pieces[2][:, :32]], axis=1)
        tail = jnp.concatenate(
            [pieces[2][r * tail_rows : (r + 1) * tail_rows, 32:] for r in range(8)], axis=1
        )
        whole = jnp.concatenate([main, tail], axis=0).astype(bf16)
        for again in range(repeat):
            send_ref[h * repeat + again] = whole


def project(repeat, my_count, embedded, slide_rows, gathered):
    rows, width = slide_rows.shape
    each = rows // DILATION
    square = jax.ShapeDtypeStruct((rows, width), bf16)
    packed = (HEADS * repeat, each + each // 8, LANES)
    return pl.pallas_call(
        functools.partial(project_kernel, repeat),
        grid=(1,),
        out_shape=[square] * 5 + [jax.ShapeDtypeStruct(packed, bf16)],
        in_specs=[
            SMEM,
            pl.BlockSpec(embedded.shape, lambda i: (0, 0, 0)),
            pl.BlockSpec((width, 2 * width), lambda i: (0, 2)),
            pl.BlockSpec((rows, width), lambda i: (0, 0)),
            pl.BlockSpec((width, 3 * width), lambda i: (0, 0)),
        ],
        out_specs=[pl.BlockSpec((rows, width), lambda i: (0, 0))] * 5
        + [pl.BlockSpec(packed, lambda i: (0, 0, 0))],
        compiler_params=PARAMS,
        cost_estimate=pl.CostEstimate(
            flops=2 * rows * width * 4 * width, bytes_accessed=16 * 1024 * 1024, transcendentals=0
        ),
        name="project",
    )(my_count, embedded, gathered, slide_rows, gathered)


def near_kernel(q_ref, k_ref, v_ref, far_ref, out_ref, lse_ref, turned, turned_far):
    rows = q_ref.shape[0]
    half = rows // 2
    chunk = 128
    turned[...] = k_ref[...].T
    turned_far[...] = far_ref[:half, :].T

    def score(h, at, in_pair):
        start, width, offset = window(h)
        lanes = slice(start, start + width)
        queries = jnp.where(lane_mask(width, offset), q_ref[at, lanes].astype(f32), 0.0).astype(bf16)
        scores = [dot(queries, turned[lanes, :])]
        if in_pair:
            scores.append(dot(queries, turned_far[lanes, :]))
        return scores

    def settle(h, at, in_pair, scores, values):
        start, width, offset = window(h)
        lanes = slice(start, start + width)
        mask = lane_mask(width, offset)
        outside = 0 if offset > 0 else HD
        peaks = [jnp.max(s, axis=1, keepdims=True) for s in scores]
        peak = functools.reduce(jnp.maximum, peaks) * SCALE
        first = h % 2 * half
        if in_pair:
            column = lax.broadcasted_iota(jnp.int32, (1, rows), 1)
            twice = jnp.where((column >= first) & (column < first + half), 1.0, 0.0)
            weights = jnp.exp2(scores[0] * SCALE - (peak - twice))
        else:
            weights = jnp.exp2(scores[0] * SCALE - peak)
        total = dot(weights.astype(bf16), values[0])
        if in_pair:
            total = total + dot(jnp.exp2(scores[1] * SCALE - peak).astype(bf16), values[1])
        mass = total[:, outside : outside + 1]
        out_ref[at, lanes] = jnp.where(mask, total * (1.0 / mass), out_ref[at, lanes])
        lse_ref[at, lanes] = jnp.where(mask, peak + jnp.log2(mass), lse_ref[at, lanes])

    waiting = None
    for h in range(8):
        start, width, offset = window(h)
        lanes = slice(start, start + width)
        mask = lane_mask(width, offset)
        values = [
            jnp.where(mask, ref.astype(f32), 1.0).astype(bf16)
            for ref in (v_ref[:, lanes], far_ref[half:, lanes])
        ]
        for part in range(rows // chunk):
            at = slice(part * chunk, (part + 1) * chunk)
            in_pair = at.start // half == h % 2
            scores = score(h, at, in_pair)
            if waiting is not None:
                settle(*waiting)
            waiting = (h, at, in_pair, scores, values)
    settle(*waiting)


def attend_near(side, queries, key_rows, value_rows, far):
    rows, width = queries.shape
    spec = pl.BlockSpec((rows, 8 * HD), lambda i: (0, side))
    return pl.pallas_call(
        near_kernel,
        grid=(1,),
        out_shape=[jax.ShapeDtypeStruct((rows, 8 * HD), f32)] * 2,
        in_specs=[spec] * 4,
        out_specs=[pl.BlockSpec((rows, 8 * HD), lambda i: (0, 0))] * 2,
        scratch_shapes=[pltpu.VMEM((8 * HD, rows), bf16), pltpu.VMEM((8 * HD, rows // 2), bf16)],
        compiler_params=PARAMS,
        cost_estimate=pl.CostEstimate(
            flops=6 * 10**9, bytes_accessed=5 * 1024 * 1024, transcendentals=6 * 10**6
        ),
        name="near_attention",
    )(queries, key_rows, value_rows, far)


def wide_kernel(repeat, part_ref, recv_ref, out_ref, keys, values, turned):
    count, packed, _ = recv_ref.shape
    each = packed * 8 // 9
    tail_rows = each // 8
    lane = lax.broadcasted_iota(jnp.int32, (1, LANES), 1)
    step = pl.program_id(0)

    @pl.when(step == 0)
    def _():
        @pl.loop(0, count)
        def _(source):
            block = recv_ref[source]
            at = pl.ds(pl.multiple_of(source * each, each), each)
            keys[at, :] = block[:each]
            wide = block.astype(f32)
            tail = wide[each:]
            tails = [tail] + [pltpu.roll(tail, LANES - 16 * r, axis=1) for r in range(1, 8)]
            tail = jnp.concatenate(tails, axis=0)
            picked = jnp.where(lane >= 96, wide[:each], jnp.where(lane < 16, tail, 1.0))
            values[at, :] = picked.astype(bf16)

        for first in range(0, count * each, 256):
            turned[:, first : first + 256] = keys[first : first + 256, :].T

    def score(index, at):
        block = recv_ref[(step * 2 + index) * repeat + part_ref[0]].astype(f32)
        queries = pltpu.roll(block[at], HD, axis=1)
        queries = jnp.where((lane >= HD) & (lane < 2 * HD), queries, 0.0).astype(bf16)
        return dot(queries, turned[...])

    def settle(scores):
        peak = jnp.max(scores, axis=1, keepdims=True) * SCALE
        total = dot(jnp.exp2(scores * SCALE - peak).astype(bf16), values[...])
        total = pltpu.roll(total, 32, axis=1)
        mass = total[:, HD : HD + 1]
        lse = peak + jnp.log2(mass)
        high, middle, low = [piece.astype(f32) for piece in split3(lse)]
        return jnp.where(
            lane < HD,
            total * (1.0 / mass),
            jnp.where(lane == HD, high, jnp.where(lane == HD + 1, middle, low)),
        )

    halves = [slice(0, each // 2), slice(each // 2, each)]
    todo = [(index, at) for index in range(2) for at in halves]
    done, waiting = [], None
    for item in todo:
        scores = score(*item)
        if waiting is not None:
            done.append(settle(waiting))
        waiting = scores
    done.append(settle(waiting))
    for index in range(2):
        upper = pltpu.roll(done[2 * index + 1], 64, axis=1)
        out_ref[index] = jnp.where(lane < 64, done[2 * index], upper).astype(bf16)


def attend_wide(repeat, part, received):
    count, packed, _ = received.shape
    each = packed * 8 // 9
    steps = count // repeat
    return pl.pallas_call(
        functools.partial(wide_kernel, repeat),
        grid=(steps // 2,),
        out_shape=jax.ShapeDtypeStruct((steps, each // 2, LANES), bf16),
        in_specs=[SMEM, pl.BlockSpec(received.shape, lambda i: (0, 0, 0))],
        out_specs=pl.BlockSpec((2, each // 2, LANES), lambda i: (i, 0, 0)),
        scratch_shapes=[pltpu.VMEM((count * each, LANES), bf16)] * 2
        + [pltpu.VMEM((LANES, count * each), bf16)],
        compiler_params=PARAMS,
        cost_estimate=pl.CostEstimate(
            flops=10 * 10**9, bytes_accessed=2 * 1024 * 1024, transcendentals=10**7
        ),
        name="wide_attention",
    )(part, received)


def finish_kernel(
    near_a_ref, lse_a_ref, near_b_ref, lse_b_ref, wide_ref, out_w_ref, now_ref, out_ref, mixed
):
    rows, width = now_ref.shape
    side = width // 2
    each = rows // DILATION
    mixed[:, :side] = near_a_ref[...]
    mixed[:, side:] = near_b_ref[...]
    for h in range(HEADS):
        near_ref, lse_ref = ((near_a_ref, lse_a_ref), (near_b_ref, lse_b_ref))[h // 8]
        start, span, offset = window(h % 8)
        lanes = slice(start, start + span)
        placed = slice(start + h // 8 * side, start + h // 8 * side + span)
        mask = lane_mask(span, offset)
        first = BLOCK_OF[h % DILATION] * each
        at = slice(first, first + each)
        block = wide_ref[h].astype(f32)
        block = jnp.concatenate([block, pltpu.roll(block, 64, axis=1)], axis=0)
        far_lse = block[:, HD : HD + 1] + block[:, HD + 1 : HD + 2] + block[:, HD + 2 : HD + 3]
        if span > LANES:
            block = jnp.concatenate([block, jnp.zeros_like(block)], axis=1)
        far_out = pltpu.roll(block, offset, axis=1) if offset else block
        near_lse = jnp.where(mask, lse_ref[at, lanes], 0.0)
        highest = jnp.maximum(near_lse, far_lse)
        near_weight, far_weight = jnp.exp2(near_lse - highest), jnp.exp2(far_lse - highest)
        merged = (near_weight * near_ref[at, lanes] + far_weight * far_out) / (near_weight + far_weight)
        mixed[at, placed] = jnp.where(mask, merged, mixed[at, placed])
    attended = dot(permutation(rows, True), mixed[...].astype(bf16)).astype(bf16)
    out_ref[...] = (now_ref[...].astype(f32) + dot(attended, out_w_ref[...])).astype(bf16)


def finish(near_a, near_b, wide, gathered, slide_now):
    rows, width = slide_now.shape
    half = pl.BlockSpec((rows, width // 2), lambda i: (0, 0))
    whole = pl.BlockSpec((rows, width), lambda i: (0, 0))
    return pl.pallas_call(
        finish_kernel,
        grid=(1,),
        out_shape=jax.ShapeDtypeStruct((rows, width), bf16),
        in_specs=[half] * 4
        + [
            pl.BlockSpec(wide.shape, lambda i: (0, 0, 0)),
            pl.BlockSpec((width, width), lambda i: (0, 3)),
            whole,
        ],
        out_specs=whole,
        scratch_shapes=[pltpu.VMEM((rows, width), f32)],
        compiler_params=PARAMS,
        cost_estimate=pl.CostEstimate(
            flops=4 * rows * width * width, bytes_accessed=9 * 1024 * 1024, transcendentals=0
        ),
        name="finish",
    )(*near_a, *near_b, wide, gathered, slide_now)


def body(tile_tokens, tile_counts, w_gate_up, w_down, w_tile_proj, slide_rows, w_qkv, w_out):
    size = lax.axis_size("slide")
    repeat = size // HEADS
    me = lax.axis_index("slide")
    my_count = lax.dynamic_slice(tile_counts, (me,), (1,))
    piece = w_qkv.shape[0]
    mine = jnp.concatenate([w_qkv, w_out, w_tile_proj[:piece], w_tile_proj[piece:]], axis=1)
    gathered = lax.all_gather(mine, "slide", axis=0, tiled=True)
    embedded = encode_tiles(my_count, tile_tokens, w_gate_up, w_down)
    keep = jnp.arange(TMAX, dtype=jnp.int32)[:, None] < my_count
    tile_embeddings = jnp.where(keep, embedded[:TMAX], jnp.zeros((), bf16))
    ordered = embedded.reshape(embedded.shape[0], size, 2, piece)
    ordered = jnp.transpose(ordered, (2, 0, 1, 3)).reshape(2, embedded.shape[0], -1)
    slide_now, queries, key_rows, value_rows, far, send = project(
        repeat, my_count, ordered, slide_rows, gathered
    )
    far = lax.ppermute(far, "slide", [(source, source ^ 1) for source in range(size)])
    received = lax.all_to_all(send, "slide", 0, 0, tiled=True)
    near_a = attend_near(0, queries, key_rows, value_rows, far)
    received, near_a = lax.optimization_barrier((received, near_a))
    wide = attend_wide(repeat, (me % repeat).astype(jnp.int32)[None], received)
    wide, queries = lax.optimization_barrier((wide, queries))
    near_b = attend_near(1, queries, key_rows, value_rows, far)
    wide = jnp.repeat(wide, repeat, axis=0) if repeat > 1 else wide
    wide = lax.all_to_all(wide, "slide", 0, 0, tiled=True)
    if repeat > 1:
        wide = lax.dynamic_index_in_dim(
            wide.reshape(HEADS, repeat, *wide.shape[1:]), me % repeat, 1, keepdims=False
        )
    return finish(near_a, near_b, wide, gathered, slide_now), tile_embeddings


def solution(mesh):
    return jax.shard_map(
        body,
        mesh=mesh,
        in_specs=(
            P(("groups", "slide"), None),
            P("groups"),
            P(),
            P(),
            P("slide", None),
            P(("groups", "slide"), None),
            P("slide", None),
            P("slide", None),
        ),
        out_specs=(P(("groups", "slide"), None), P(("groups", "slide"), None)),
        check_vma=False,
    )
```

```python
import functools
import math

import jax
import jax.numpy as jnp
import numpy as np
from jax import lax
from jax.experimental import pallas as pl
from jax.experimental.pallas import tpu as pltpu
from jax.sharding import PartitionSpec as P

TT = 256
TMAX = 3
HEADS = 16
HD = 48
DILATION = 4
LANES = 128

tile_epsilon = 1e-06
slide_epsilon = 1e-05
SCALE = HD ** (-0.5) * math.log2(math.e)
BLOCK_OF = {0: 0, 2: 1, 1: 2, 3: 3}

f32 = jnp.float32
bf16 = jnp.bfloat16
VMEM = pl.BlockSpec(memory_space=pltpu.VMEM)
SMEM = pl.BlockSpec(memory_space=pltpu.SMEM)
PARAMS = pltpu.CompilerParams(vmem_limit_bytes=56 * 1024 * 1024)


def normalize(matrix, epsilon):
    average = jnp.mean(matrix, axis=-1, keepdims=True)
    centered = matrix - average
    variance = jnp.mean(centered * centered, axis=-1, keepdims=True)
    return centered * lax.rsqrt(variance + epsilon)


def dot(a, b):
    return jnp.dot(a, b, preferred_element_type=f32)


def dot_nt(a, b):
    return lax.dot_general(a, b, (((1,), (1,)), ((), ())), preferred_element_type=f32)


def split3(value):
    high = value.astype(bf16)
    rest = value - high.astype(f32)
    middle = rest.astype(bf16)
    return high, middle, (rest - middle.astype(f32)).astype(bf16)


def window(head):
    first = head * HD
    start = first // LANES * LANES
    width = LANES if first + HD <= start + LANES else 2 * LANES
    return start, width, first - start


def lane_mask(width, offset):
    lane = lax.broadcasted_iota(jnp.int32, (1, width), 1)
    return (lane >= offset) & (lane < offset + HD)


def permutation(rows, transposed):
    each = rows // DILATION
    stored = lax.broadcasted_iota(jnp.int32, (rows, rows), 1 if transposed else 0)
    position = lax.broadcasted_iota(jnp.int32, (rows, rows), 0 if transposed else 1)
    block = sum((stored >= each * i).astype(jnp.int32) for i in range(1, DILATION))
    phase = jnp.where(block == 1, 2, jnp.where(block == 2, 1, block))
    wanted = (stored - block * each) * DILATION + phase
    return jnp.where(position == wanted, 1.0, 0.0).astype(bf16)


def tile_kernel(count_ref, tokens_ref, gate_ref, up_ref, down_ref, out_ref, normed, mixed):
    step = pl.program_id(0)

    @pl.when(step == 0)
    def _():
        mixed[...] = jnp.zeros_like(mixed)
        for slot in range(TMAX):
            rows = pl.ds(slot * TT, TT)
            tokens = tokens_ref[rows, :].astype(f32)
            normed[rows, :] = normalize(tokens, tile_epsilon).astype(bf16)
            mixed[slot : slot + 1, :] = jnp.sum(tokens, axis=0, keepdims=True)

    for slot in range(TMAX):

        @pl.when(slot < count_ref[0])
        def _():
            rows = normed[pl.ds(slot * TT, TT), :]
            gate = dot(rows, gate_ref[...])
            up = dot(rows, up_ref[...])
            hidden = (gate * jax.nn.sigmoid(gate) * up).astype(bf16).astype(f32)
            total = jnp.broadcast_to(jnp.sum(hidden, axis=0, keepdims=True), (8, hidden.shape[1]))
            parts = split3(total)
            down = down_ref[...]
            add = dot(parts[0], down) + dot(parts[1], down) + dot(parts[2], down)
            mixed[slot : slot + 1, :] += add[:1]

    @pl.when(step == pl.num_programs(0) - 1)
    def _():
        out_ref[...] = normalize(mixed[...] / TT, tile_epsilon).astype(bf16)


def encode_tiles(my_count, tile_tokens, w_gate_up, w_down):
    rows, width = tile_tokens.shape
    hidden = w_down.shape[0]
    block = 512
    steps = hidden // block
    return pl.pallas_call(
        tile_kernel,
        grid=(steps,),
        out_shape=jax.ShapeDtypeStruct((16, width), bf16),
        in_specs=[
            SMEM,
            pl.BlockSpec((rows, width), lambda i: (0, 0)),
            pl.BlockSpec((width, block), lambda i: (0, i)),
            pl.BlockSpec((width, block), lambda i: (0, i + steps)),
            pl.BlockSpec((block, width), lambda i: (i, 0)),
        ],
        out_specs=pl.BlockSpec((16, width), lambda i: (0, 0)),
        scratch_shapes=[pltpu.VMEM((rows, width), bf16), pltpu.VMEM((16, width), f32)],
        compiler_params=PARAMS,
        cost_estimate=pl.CostEstimate(
            flops=2 * rows * width * 2 * hidden, bytes_accessed=22 * 1024 * 1024, transcendentals=0
        ),
        name="tile_block",
    )(my_count, tile_tokens, w_gate_up, w_gate_up, w_down)


def project_kernel(
    repeat, count_ref, fresh_ref, rows_ref, qkv_ref, now_ref, q_ref, k_ref, v_ref, far_ref, send_ref
):
    rows, width = rows_ref.shape
    each, half = rows // DILATION, rows // 2
    fresh = fresh_ref[...].astype(f32)
    keep = lax.broadcasted_iota(jnp.int32, (16, 1), 0) < count_ref[0]
    now_ref[...] = rows_ref[...]
    now_ref[0:16, :] = jnp.where(keep, fresh, rows_ref[0:16, :].astype(f32)).astype(bf16)
    normed = normalize(now_ref[...].astype(f32), slide_epsilon).astype(bf16)
    normed = dot(permutation(rows, False), normed).astype(bf16)
    for index, ref in enumerate((q_ref, k_ref, v_ref)):
        ref[...] = dot(normed, qkv_ref[:, index * width : (index + 1) * width]).astype(bf16)
    lane = lax.broadcasted_iota(jnp.int32, (1, width), 1)
    head = sum((lane >= HD * i).astype(jnp.int32) for i in range(1, HEADS))
    even = (head & 1) == 0
    for index, ref in enumerate((k_ref, v_ref)):
        far_ref[index * half : (index + 1) * half, :] = jnp.where(
            even, ref[0:half, :].astype(f32), ref[half:rows, :].astype(f32)
        ).astype(bf16)
    tail_rows = each // 8
    for h in range(HEADS):
        first = BLOCK_OF[h % DILATION] * each
        pieces = [
            ref[first : first + each, h * HD : (h + 1) * HD].astype(f32)
            for ref in (q_ref, k_ref, v_ref)
        ]
        main = jnp.concatenate([pieces[0], pieces[1], pieces[2][:, :32]], axis=1)
        tail = jnp.concatenate(
            [pieces[2][r * tail_rows : (r + 1) * tail_rows, 32:] for r in range(8)], axis=1
        )
        whole = jnp.concatenate([main, tail], axis=0).astype(bf16)
        for again in range(repeat):
            send_ref[h * repeat + again] = whole


def project(repeat, my_count, fresh, slide_rows, qkv_full):
    rows, width = slide_rows.shape
    each = rows // DILATION
    square = jax.ShapeDtypeStruct((rows, width), bf16)
    packed = (HEADS * repeat, each + each // 8, LANES)
    return pl.pallas_call(
        functools.partial(project_kernel, repeat),
        grid=(1,),
        out_shape=[square] * 5 + [jax.ShapeDtypeStruct(packed, bf16)],
        in_specs=[
            SMEM,
            pl.BlockSpec(fresh.shape, lambda i: (0, 0)),
            pl.BlockSpec((rows, width), lambda i: (0, 0)),
            pl.BlockSpec((width, 3 * width), lambda i: (0, 0)),
        ],
        out_specs=[pl.BlockSpec((rows, width), lambda i: (0, 0))] * 5
        + [pl.BlockSpec(packed, lambda i: (0, 0, 0))],
        compiler_params=PARAMS,
        cost_estimate=pl.CostEstimate(
            flops=2 * rows * width * 4 * width, bytes_accessed=16 * 1024 * 1024, transcendentals=0
        ),
        name="project",
    )(my_count, fresh, slide_rows, qkv_full)


def near_kernel(q_ref, k_ref, v_ref, far_ref, out_ref, lse_ref, turned, turned_far):
    rows = q_ref.shape[0]
    half = rows // 2
    chunk = 128
    turned[...] = k_ref[...].T
    turned_far[...] = far_ref[:half, :].T

    def score(h, at, in_pair):
        start, width, offset = window(h)
        lanes = slice(start, start + width)
        queries = jnp.where(lane_mask(width, offset), q_ref[at, lanes].astype(f32), 0.0).astype(bf16)
        scores = [dot(queries, turned[lanes, :])]
        if in_pair:
            scores.append(dot(queries, turned_far[lanes, :]))
        return scores

    def settle(h, at, in_pair, scores, values):
        start, width, offset = window(h)
        lanes = slice(start, start + width)
        mask = lane_mask(width, offset)
        outside = 0 if offset > 0 else HD
        peaks = [jnp.max(s, axis=1, keepdims=True) for s in scores]
        peak = functools.reduce(jnp.maximum, peaks) * SCALE
        first = h % 2 * half
        if in_pair:
            column = lax.broadcasted_iota(jnp.int32, (1, rows), 1)
            twice = jnp.where((column >= first) & (column < first + half), 1.0, 0.0)
            weights = jnp.exp2(scores[0] * SCALE - (peak - twice))
        else:
            weights = jnp.exp2(scores[0] * SCALE - peak)
        total = dot(weights.astype(bf16), values[0])
        if in_pair:
            total = total + dot(jnp.exp2(scores[1] * SCALE - peak).astype(bf16), values[1])
        mass = total[:, outside : outside + 1]
        out_ref[at, lanes] = jnp.where(mask, total * (1.0 / mass), out_ref[at, lanes])
        lse_ref[at, lanes] = jnp.where(mask, peak + jnp.log2(mass), lse_ref[at, lanes])

    waiting = None
    for h in range(8):
        start, width, offset = window(h)
        lanes = slice(start, start + width)
        mask = lane_mask(width, offset)
        values = [
            jnp.where(mask, ref.astype(f32), 1.0).astype(bf16)
            for ref in (v_ref[:, lanes], far_ref[half:, lanes])
        ]
        for part in range(rows // chunk):
            at = slice(part * chunk, (part + 1) * chunk)
            in_pair = at.start // half == h % 2
            scores = score(h, at, in_pair)
            if waiting is not None:
                settle(*waiting)
            waiting = (h, at, in_pair, scores, values)
    settle(*waiting)


def attend_near(side, queries, key_rows, value_rows, far):
    rows, width = queries.shape
    spec = pl.BlockSpec((rows, 8 * HD), lambda i: (0, side))
    return pl.pallas_call(
        near_kernel,
        grid=(1,),
        out_shape=[jax.ShapeDtypeStruct((rows, 8 * HD), f32)] * 2,
        in_specs=[spec] * 4,
        out_specs=[pl.BlockSpec((rows, 8 * HD), lambda i: (0, 0))] * 2,
        scratch_shapes=[pltpu.VMEM((8 * HD, rows), bf16), pltpu.VMEM((8 * HD, rows // 2), bf16)],
        compiler_params=PARAMS,
        cost_estimate=pl.CostEstimate(
            flops=6 * 10**9, bytes_accessed=5 * 1024 * 1024, transcendentals=6 * 10**6
        ),
        name="near_attention",
    )(queries, key_rows, value_rows, far)


def wide_kernel(repeat, part_ref, recv_ref, out_ref, keys, values, turned):
    count, packed, _ = recv_ref.shape
    each = packed * 8 // 9
    tail_rows = each // 8
    lane = lax.broadcasted_iota(jnp.int32, (1, LANES), 1)
    step = pl.program_id(0)

    @pl.when(step == 0)
    def _():
        @pl.loop(0, count)
        def _(source):
            block = recv_ref[source]
            at = pl.ds(pl.multiple_of(source * each, each), each)
            keys[at, :] = block[:each]
            wide = block.astype(f32)
            tail = wide[each:]
            tails = [tail] + [pltpu.roll(tail, LANES - 16 * r, axis=1) for r in range(1, 8)]
            tail = jnp.concatenate(tails, axis=0)
            picked = jnp.where(lane >= 96, wide[:each], jnp.where(lane < 16, tail, 1.0))
            values[at, :] = picked.astype(bf16)

        for first in range(0, count * each, 256):
            turned[:, first : first + 256] = keys[first : first + 256, :].T

    def score(index, at):
        block = recv_ref[(step * 2 + index) * repeat + part_ref[0]].astype(f32)
        queries = pltpu.roll(block[at], HD, axis=1)
        queries = jnp.where((lane >= HD) & (lane < 2 * HD), queries, 0.0).astype(bf16)
        return dot(queries, turned[...])

    def settle(scores):
        peak = jnp.max(scores, axis=1, keepdims=True) * SCALE
        total = dot(jnp.exp2(scores * SCALE - peak).astype(bf16), values[...])
        total = pltpu.roll(total, 32, axis=1)
        mass = total[:, HD : HD + 1]
        lse = peak + jnp.log2(mass)
        high, middle, low = [piece.astype(f32) for piece in split3(lse)]
        return jnp.where(
            lane < HD,
            total * (1.0 / mass),
            jnp.where(lane == HD, high, jnp.where(lane == HD + 1, middle, low)),
        )

    halves = [slice(0, each // 2), slice(each // 2, each)]
    todo = [(index, at) for index in range(2) for at in halves]
    done, waiting = [], None
    for item in todo:
        scores = score(*item)
        if waiting is not None:
            done.append(settle(waiting))
        waiting = scores
    done.append(settle(waiting))
    for index in range(2):
        upper = pltpu.roll(done[2 * index + 1], 64, axis=1)
        out_ref[index] = jnp.where(lane < 64, done[2 * index], upper).astype(bf16)


def attend_wide(repeat, part, received):
    count, packed, _ = received.shape
    each = packed * 8 // 9
    steps = count // repeat
    return pl.pallas_call(
        functools.partial(wide_kernel, repeat),
        grid=(steps // 2,),
        out_shape=jax.ShapeDtypeStruct((steps, each // 2, LANES), bf16),
        in_specs=[SMEM, pl.BlockSpec(received.shape, lambda i: (0, 0, 0))],
        out_specs=pl.BlockSpec((2, each // 2, LANES), lambda i: (i, 0, 0)),
        scratch_shapes=[pltpu.VMEM((count * each, LANES), bf16)] * 2
        + [pltpu.VMEM((LANES, count * each), bf16)],
        compiler_params=PARAMS,
        cost_estimate=pl.CostEstimate(
            flops=10 * 10**9, bytes_accessed=2 * 1024 * 1024, transcendentals=10**7
        ),
        name="wide_attention",
    )(part, received)


def finish_kernel(
    near_a_ref, lse_a_ref, near_b_ref, lse_b_ref, wide_ref, out_w_ref, now_ref, out_ref, mixed
):
    rows, width = now_ref.shape
    side = width // 2
    each = rows // DILATION
    mixed[:, :side] = near_a_ref[...]
    mixed[:, side:] = near_b_ref[...]
    for h in range(HEADS):
        near_ref, lse_ref = ((near_a_ref, lse_a_ref), (near_b_ref, lse_b_ref))[h // 8]
        start, span, offset = window(h % 8)
        lanes = slice(start, start + span)
        placed = slice(start + h // 8 * side, start + h // 8 * side + span)
        mask = lane_mask(span, offset)
        first = BLOCK_OF[h % DILATION] * each
        at = slice(first, first + each)
        block = wide_ref[h].astype(f32)
        block = jnp.concatenate([block, pltpu.roll(block, 64, axis=1)], axis=0)
        far_lse = block[:, HD : HD + 1] + block[:, HD + 1 : HD + 2] + block[:, HD + 2 : HD + 3]
        if span > LANES:
            block = jnp.concatenate([block, jnp.zeros_like(block)], axis=1)
        far_out = pltpu.roll(block, offset, axis=1) if offset else block
        near_lse = jnp.where(mask, lse_ref[at, lanes], 0.0)
        highest = jnp.maximum(near_lse, far_lse)
        near_weight, far_weight = jnp.exp2(near_lse - highest), jnp.exp2(far_lse - highest)
        merged = (near_weight * near_ref[at, lanes] + far_weight * far_out) / (near_weight + far_weight)
        mixed[at, placed] = jnp.where(mask, merged, mixed[at, placed])
    attended = dot(permutation(rows, True), mixed[...].astype(bf16)).astype(bf16)
    out_ref[...] = (now_ref[...].astype(f32) + dot(attended, out_w_ref[...])).astype(bf16)


def finish(near_a, near_b, wide, out_full, slide_now):
    rows, width = slide_now.shape
    half = pl.BlockSpec((rows, width // 2), lambda i: (0, 0))
    whole = pl.BlockSpec((rows, width), lambda i: (0, 0))
    return pl.pallas_call(
        finish_kernel,
        grid=(1,),
        out_shape=jax.ShapeDtypeStruct((rows, width), bf16),
        in_specs=[half] * 4
        + [
            pl.BlockSpec(wide.shape, lambda i: (0, 0, 0)),
            pl.BlockSpec((width, width), lambda i: (0, 0)),
            whole,
        ],
        out_specs=whole,
        scratch_shapes=[pltpu.VMEM((rows, width), f32)],
        compiler_params=PARAMS,
        cost_estimate=pl.CostEstimate(
            flops=4 * rows * width * width, bytes_accessed=9 * 1024 * 1024, transcendentals=0
        ),
        name="finish",
    )(*near_a, *near_b, wide, out_full, slide_now)


def body(tile_tokens, tile_counts, w_gate_up, w_down, w_tile_proj, slide_rows, w_qkv, w_out):
    size = lax.axis_size("slide")
    repeat = size // HEADS
    me = lax.axis_index("slide")
    my_count = lax.dynamic_slice(tile_counts, (me,), (1,))
    qkv_full = lax.all_gather(w_qkv, "slide", axis=0, tiled=True)
    w_out, qkv_full = lax.optimization_barrier((w_out, qkv_full))
    out_full = lax.all_gather(w_out, "slide", axis=0, tiled=True)
    embedded = encode_tiles(my_count, tile_tokens, w_gate_up, w_down)
    keep = jnp.arange(TMAX, dtype=jnp.int32)[:, None] < my_count
    tile_embeddings = jnp.where(keep, embedded[:TMAX], jnp.zeros((), bf16))
    piece, slide_width = w_tile_proj.shape
    shares = jnp.transpose(embedded.reshape(-1, size, piece), (1, 0, 2))
    shares = lax.all_to_all(shares, "slide", 0, 0, tiled=True)
    terms = dot(shares.reshape(-1, piece), w_tile_proj).reshape(size, -1, slide_width)
    terms = terms[:, :TMAX].reshape(size, -1, LANES)
    terms = lax.all_to_all(terms, "slide", 0, 0, tiled=True)
    fresh = jnp.sum(terms, axis=0).reshape(TMAX, slide_width).astype(bf16)
    fresh = jnp.pad(fresh, ((0, 16 - TMAX), (0, 0)))
    slide_now, queries, key_rows, value_rows, far, send = project(
        repeat, my_count, fresh, slide_rows, qkv_full
    )
    far = lax.ppermute(far, "slide", [(source, source ^ 1) for source in range(size)])
    received = lax.all_to_all(send, "slide", 0, 0, tiled=True)
    near_a = attend_near(0, queries, key_rows, value_rows, far)
    received, near_a = lax.optimization_barrier((received, near_a))
    wide = attend_wide(repeat, (me % repeat).astype(jnp.int32)[None], received)
    wide, queries = lax.optimization_barrier((wide, queries))
    near_b = attend_near(1, queries, key_rows, value_rows, far)
    wide = jnp.repeat(wide, repeat, axis=0) if repeat > 1 else wide
    wide = lax.all_to_all(wide, "slide", 0, 0, tiled=True)
    if repeat > 1:
        wide = lax.dynamic_index_in_dim(
            wide.reshape(HEADS, repeat, *wide.shape[1:]), me % repeat, 1, keepdims=False
        )
    return finish(near_a, near_b, wide, out_full, slide_now), tile_embeddings


def solution(mesh):
    return jax.shard_map(
        body,
        mesh=mesh,
        in_specs=(
            P(("groups", "slide"), None),
            P("groups"),
            P(),
            P(),
            P("slide", None),
            P(("groups", "slide"), None),
            P("slide", None),
            P("slide", None),
        ),
        out_specs=(P(("groups", "slide"), None), P(("groups", "slide"), None)),
        check_vma=False,
    )
```
